32 devices in a mesh: lat: 8 (over z, x), lev: 4 (over y, core).
Axes of the slice: x: 2, y: 2, z: 4, core: 2. Of those that a mesh axis runs over, the one named last changes fastest.
Arguments:
- spectral: bfloat16 [1280, 1280, 64], P('lat', 'lev'), may hold values from -0.0048828125 to 0.0048828125
- legendre: bfloat16 [1280, 1280, 32], P('lat', 'lev'), may hold values from -6 to 6
- weights: float32 [16], P('lat'), may hold values from 4 to 40
- points: int32 [8], P('lat'), may hold values from 20 to 5136, as said below
- assignment: int32 [1280], replicated, may hold values from 0 to 1279, each once
Outputs:
- tendency: bfloat16 [1280, 1280, 64], P('lat', 'lev')
- grid_values: bfloat16 [16, 8, 4, 5376], P('lat', 'lev')
The draws below stay inside these ranges and needn't reach their ends.
Inputs may be any that keep to these rules, and one draw needn't show every extreme that they name: `assignment`: each of the 1280 wavenumbers appears once; slot k lies with lat index k // 160. `points`: each value is 20 + 4 i for a row index i from 0 to 1279; some pair has 20 points and some pair 4 * 1280 + 16.
All inputs are finite; a program needn't handle non-finite values.
Results may differ from the reference program's by a relative error of at most 0.03.
Values may be sent and summed in bfloat16 or wider, within the bound.
A program may use at most 64 MiB of HBM per device.

```python
import math
import jax
import jax.numpy as jnp
from jax import lax

M = 1280
N = 1280
PAIRS = 8
LATS = 16
LT = 32
COLS = 64
NPAD = 5376
N_LEV = 4


def draw_points(key, part):
    key = jax.random.fold_in(key, 7)
    first_key, second_key = jax.random.split(key)
    row_index = jax.random.randint(first_key, (PAIRS,), 0, M)
    places = jax.random.permutation(second_key, PAIRS)
    row_index = row_index.at[places[0]].set(M - 1)
    row_index = row_index.at[places[1]].set(0)
    return (20 + 4 * row_index).astype(jnp.int32)


def block_levels(own_key, shape, cuts, smallest, high):
    gain, own = 1.0, jax.random.fold_in(own_key, 6)
    for axis_at, shards_of in cuts:
        draws = jnp.exp(jax.random.uniform(jax.random.fold_in(own, axis_at), (shards_of,), jnp.float32, smallest / len(cuts), high / len(cuts)))
        gain = gain * jnp.repeat(draws, shape[axis_at] // shards_of).reshape([-1 if axis == axis_at else 1 for axis in range(len(shape))])
    return gain


def noise(stream_key, shape, scale, reach, cuts=(), kind=jnp.bfloat16):
    array = scale * jax.random.normal(stream_key, shape, jnp.float32)
    if cuts:
        array = array * block_levels(stream_key, shape, cuts, -0.22, 0.18)
    return jnp.clip(array, -reach, reach).astype(kind)


def setup_inputs(seed: int = 0) -> dict:
    arg_keys = jax.random.split(jax.random.key(seed), 6)
    spectral = noise(arg_keys[0], (M, N, COLS), (M * N) ** -0.5, 0.0048828125, ((0, 8), (1, 4)))
    legendre = noise(arg_keys[1], (M, N, LT), 1.0, 6.0, ((0, 8), (1, 4)))
    weights = jnp.clip(jnp.exp(math.log(40.0) - 2.3025851 * jax.random.uniform(arg_keys[2], (LATS,), jnp.float32) ** block_levels(arg_keys[2], (LATS,), ((0, 8),), -0.2, 0.2)), 4.0, 40.0)
    points = draw_points(jax.random.fold_in(arg_keys[5], 71), 0)
    assignment = jax.random.permutation(arg_keys[4], M).astype(jnp.int32)
    return {"spectral": spectral, "legendre": legendre, "weights": weights, "points": points, "assignment": assignment}


def fourier_table(wavenums, row_points, first_column, width):
    columns = first_column + jnp.arange(width, dtype=jnp.int32)
    residue = (wavenums[:, None] * columns[None, :]) % row_points
    angles = residue.astype(jnp.float32) * (2.0 * math.pi / row_points.astype(jnp.float32))
    active = (2 * wavenums[:, None] < row_points) & (columns[None, :] < row_points)
    cosine_rows = jnp.where(active, jnp.cos(angles), 0.0).astype(jnp.bfloat16)
    sine_rows = jnp.where(active, jnp.sin(angles), 0.0).astype(jnp.bfloat16)
    return jnp.concatenate([cosine_rows, sine_rows], axis=0)


def inverse_coefs(real_value, imag_value, real_slope, imag_slope, wavenums):
    truncation = wavenums.shape[0]
    factor = jnp.where(wavenums == 0, 1.0, 2.0).astype(jnp.float32)
    scaled_m = wavenums.astype(jnp.float32) / truncation
    cosine_part = jnp.stack([factor * real_value, -factor * scaled_m * imag_value, factor * real_slope], axis=1)
    sine_part = jnp.stack([-factor * imag_value, -factor * scaled_m * real_value, -factor * imag_slope], axis=1)
    return jnp.concatenate([cosine_part, sine_part], axis=-1).astype(jnp.bfloat16)


def grid_products(grid_field, scales):
    value_field = grid_field[:, 0]
    zonal_slope = grid_field[:, 1]
    merid_slope = grid_field[:, 2]
    advect = jnp.roll(value_field, -1, axis=2) * zonal_slope + jnp.roll(value_field, -2, axis=2) * merid_slope
    product = value_field * jnp.roll(value_field, -3, axis=2)
    terms = jnp.stack([advect, product], axis=1) * scales[:, None, None, None, None]
    return value_field.astype(jnp.bfloat16), terms.astype(jnp.bfloat16)


def direct_parts(spectra, wave_count):
    real_part = spectra[:, :wave_count]
    imag_part = -spectra[:, wave_count:]
    shape_out = (2, 2, -1, 4, wave_count)
    return jnp.stack([real_part.reshape(shape_out), imag_part.reshape(shape_out)], axis=3).astype(jnp.bfloat16)


def reference(spectral, legendre, weights, points, assignment):
    wave_count, total_count, column_count = spectral.shape
    levels = column_count // 8
    block_size = total_count // N_LEV
    triangle = jnp.arange(total_count, dtype=jnp.int32)[None, :] >= assignment[:, None]
    masked = jnp.where(triangle[:, :, None], spectral, jnp.zeros((), spectral.dtype))

    def inverse_row(operands):
        row_spec, row_table = operands
        coefs_row = row_spec.astype(jnp.float32).reshape(N_LEV, block_size, column_count)
        table_row = row_table.astype(jnp.float32).reshape(N_LEV, block_size, -1)
        blocks = jnp.einsum('bnt,bnc->btc', table_row, coefs_row)
        rounded = lax.optimization_barrier(blocks.astype(jnp.bfloat16))
        return jnp.sum(rounded.astype(jnp.float32), axis=0)

    fourier = lax.map(inverse_row, (masked, legendre))
    pair_count = points.shape[0]
    grouped = jnp.moveaxis(fourier.reshape(wave_count, pair_count, 4, column_count), 1, 0)

    def pair_work(operands):
        block_four, row_points, pair_weights = operands
        components = block_four.reshape(wave_count, 2, 2, levels, 2, 4)

        def select(deriv, half):
            return jnp.moveaxis(components[:, :, deriv, :, half, :], 0, -1)

        coefs = inverse_coefs(select(0, 0), select(0, 1), select(1, 0), select(1, 1), assignment)
        basis = fourier_table(assignment, row_points, 0, NPAD)
        grid_field = jnp.dot(coefs.reshape(-1, 2 * wave_count), basis, preferred_element_type=jnp.float32)
        grid_field = grid_field.reshape(2, 3, levels, 4, NPAD)
        values, terms = grid_products(grid_field, pair_weights / row_points.astype(jnp.float32))
        spectra = lax.dot_general(terms.reshape(-1, NPAD), basis, (((1,), (1,)), ((), ())), preferred_element_type=jnp.float32)
        wave_data = direct_parts(spectra, wave_count)
        return values, jnp.transpose(wave_data, (5, 0, 1, 2, 3, 4)).reshape(wave_count, 4, column_count)

    values, wave_data = lax.map(pair_work, (grouped, points, weights.reshape(pair_count, 2)))
    grid_values = values.reshape(2 * pair_count, levels, 4, NPAD)
    wave_data = jnp.moveaxis(wave_data, 0, 1).reshape(wave_count, 4 * pair_count, column_count)

    def direct_row(operands):
        row_table, row_waves = operands
        return jnp.dot(row_table, row_waves, preferred_element_type=jnp.float32)

    result = lax.map(direct_row, (legendre, wave_data))
    tendency = jnp.where(triangle[:, :, None], result, 0.0).astype(jnp.bfloat16)
    return tendency, grid_values
```

```python
import math

import jax
import jax.numpy as jnp
from jax import lax
from jax.experimental import pallas as pl
from jax.experimental.pallas import tpu as pltpu
from jax.sharding import PartitionSpec as P

NPAD = 5376
LANE = 128


def sincos(product, quarter, step):
    turns = jnp.floor(product * (1.0 / quarter) + 0.5)
    theta = (product - turns * quarter) * step
    square = theta * theta
    sine = theta * (1.0 + square * (-1.0 / 6 + square * (1.0 / 120 - square * (1.0 / 5040))))
    cosine = 1.0 + square * (-0.5 + square * (1.0 / 24 + square * (-1.0 / 720 + square * (1.0 / 40320))))
    quadrant = turns.astype(jnp.int32) & 3
    odd = (quadrant & 1) == 1
    first = jnp.where(odd, sine, cosine)
    second = jnp.where(odd, cosine, sine)
    return (
        jnp.where((quadrant == 1) | (quadrant == 2), -first, first),
        jnp.where(quadrant >= 2, -second, second),
    )


def shift_field(rows, shift):
    count = rows.shape[0]
    field = lax.broadcasted_iota(jnp.int32, rows.shape, 0) % 4
    return jnp.where(
        field < 4 - shift,
        pltpu.roll(rows, count - shift, axis=0),
        pltpu.roll(rows, 4 - shift, axis=0),
    )


def grid_kernel(
    points_ref, scales_ref, waves_ref, four_ref, out_ref, values_ref,
    base_cos, base_sin, start_cos, start_sin, cos_tab, sin_tab, lhs_cos, lhs_sin, term_cos, term_sin, images,
):
    width = cos_tab.shape[0]
    wave_count = cos_tab.shape[1]
    rows = four_ref.shape[1]
    blocks = width // LANE
    row_points = points_ref[0]
    quarter_int = row_points // 4
    quarter = quarter_int.astype(jnp.float32)
    step = (0.5 * math.pi) / quarter
    m_int = waves_ref[...]
    m_float = m_int.astype(jnp.float32)

    def start_rows(count, scale):
        return (lax.broadcasted_iota(jnp.int32, (count, 1), 0) * scale).astype(jnp.float32)

    start_cos[...], start_sin[...] = sincos(start_rows(start_cos.shape[0], LANE) * m_float, quarter, step)

    @pl.loop(0, LANE // 8)
    def _(index):
        at = pl.multiple_of(index * 8, 8)
        offsets = (lax.broadcasted_iota(jnp.int32, (8, 1), 0) + at).astype(jnp.float32)
        base_cos[pl.ds(at, 8), :], base_sin[pl.ds(at, 8), :] = sincos(offsets * m_float, quarter, step)

    @pl.loop(0, width // 16)
    def _(index):
        at = pl.multiple_of(index * 16, 16)
        low = pl.multiple_of((index % (LANE // 16)) * 16, 16)
        start = index // (LANE // 16)
        for col in range(0, wave_count, 2 * LANE):
            cols = pl.ds(col, 2 * LANE)
            bc = base_cos[pl.ds(low, 16), cols]
            bs = base_sin[pl.ds(low, 16), cols]
            sc = start_cos[pl.ds(start, 1), cols]
            ss = start_sin[pl.ds(start, 1), cols]
            cos_tab[pl.ds(at, 16), cols] = (sc * bc - ss * bs).astype(jnp.bfloat16)
            sin_tab[pl.ds(at, 16), cols] = (ss * bc + sc * bs).astype(jnp.bfloat16)

    active = 2 * m_int < row_points
    parity = jnp.where((m_int & 1) == 0, 1.0, -1.0)
    factor = jnp.where(active, jnp.where(m_int == 0, 1.0, 2.0), 0.0)
    slope = factor * (m_float * (1.0 / wave_count))
    real_value, imag_value = four_ref[0].astype(jnp.float32), four_ref[1].astype(jnp.float32)
    real_slope, imag_slope = four_ref[2].astype(jnp.float32), four_ref[3].astype(jnp.float32)

    def fill(lhs, value, zonal, merid):
        parts = [value, shift_field(value, 1), shift_field(value, 2), shift_field(value, 3), zonal, merid]
        for index, part in enumerate(parts):
            lhs[pl.ds(index * rows, rows), :] = part.astype(jnp.bfloat16)
            lhs[pl.ds((6 + index) * rows, rows), :] = (part * parity).astype(jnp.bfloat16)

    fill(lhs_cos, factor * real_value, -slope * imag_value, factor * real_slope)
    fill(lhs_sin, -factor * imag_value, -slope * real_value, -factor * imag_slope)
    scale = scales_ref[...]

    @pl.loop(0, blocks)
    def _(index):
        at = pl.multiple_of(index * LANE, LANE)
        contract = (((1,), (1,)), ((), ()))
        even = lax.dot_general(lhs_cos[...], cos_tab[pl.ds(at, LANE), :], contract, preferred_element_type=jnp.float32)
        odd = lax.dot_general(lhs_sin[...], sin_tab[pl.ds(at, LANE), :], contract, preferred_element_type=jnp.float32)
        place = lax.broadcasted_iota(jnp.int32, (1, LANE), 1) + at
        closed = place <= quarter_int
        inner = (place >= 1) & (place < quarter_int)
        half = 6 * rows
        fields = (
            (even[:half] + odd[:half], closed),
            (even[half:] + odd[half:], closed),
            (even[half:] - odd[half:], inner),
            (even[:half] - odd[:half], inner),
        )
        terms = []
        for image, (field, keep) in enumerate(fields):
            q0, q1, q2, q3, zonal, merid = (field[part * rows:(part + 1) * rows] for part in range(6))
            images[image, :, pl.ds(at, LANE)] = jnp.where(keep, q0, 0.0)
            weight = jnp.where(keep, scale, 0.0)
            terms.append(jnp.concatenate([(q1 * zonal + q2 * merid) * weight, q0 * q3 * weight], axis=0))
        cols = pl.ds(at, LANE)
        term_cos[:, cols] = jnp.concatenate([terms[0] + terms[3], terms[1] + terms[2]], axis=0).astype(jnp.bfloat16)
        term_sin[:, cols] = jnp.concatenate([terms[0] - terms[3], terms[1] - terms[2]], axis=0).astype(jnp.bfloat16)

    keep_wave = jnp.where(active, 1.0, 0.0)
    real = jnp.dot(term_cos[...], cos_tab[...], preferred_element_type=jnp.float32)
    imag = jnp.dot(term_sin[...], sin_tab[...], preferred_element_type=jnp.float32)
    split = 2 * rows
    out_ref[0] = ((real[:split] + parity * real[split:]) * keep_wave).astype(out_ref.dtype)
    out_ref[1] = (-(imag[:split] + parity * imag[split:]) * keep_wave).astype(out_ref.dtype)

    flip = (
        lax.broadcasted_iota(jnp.int32, (LANE, LANE), 0) + lax.broadcasted_iota(jnp.int32, (LANE, LANE), 1) == LANE - 1
    ).astype(jnp.float32).astype(jnp.bfloat16)
    pad = jnp.zeros((rows, NPAD - width), jnp.float32)

    def reverse(image):
        parts = [
            jnp.dot(images[image, :, pl.ds(block * LANE, LANE)].astype(jnp.bfloat16), flip, preferred_element_type=jnp.float32)
            for block in reversed(range(blocks))
        ]
        return jnp.concatenate(parts + [pad], axis=1)

    def straight(image):
        return jnp.concatenate([images[image], pad], axis=1)

    halfway = row_points // 2
    total = straight(0)
    total = total + pltpu.roll(straight(1), halfway, axis=1)
    total = total + pltpu.roll(reverse(2), lax.rem(halfway - (width - 1) + NPAD, NPAD), axis=1)
    total = total + pltpu.roll(reverse(3), lax.rem(row_points - (width - 1) + NPAD, NPAD), axis=1)
    values_ref[...] = total.astype(values_ref.dtype)


def grid_stage(four, scales, row_points, assignment):
    _, rows, wave_count = four.shape
    width = -(-(wave_count + 5) // LANE) * LANE
    starts = -(-(width // LANE) // 8) * 8
    smem, vmem = pl.BlockSpec(memory_space=pltpu.SMEM), pl.BlockSpec(memory_space=pltpu.VMEM)
    f32, b16 = jnp.float32, jnp.bfloat16
    return pl.pallas_call(
        grid_kernel,
        out_shape=(jax.ShapeDtypeStruct((2, 2 * rows, wave_count), b16), jax.ShapeDtypeStruct((rows, NPAD), b16)),
        in_specs=[smem, vmem, vmem, vmem],
        out_specs=(vmem, vmem),
        scratch_shapes=[
            pltpu.VMEM((LANE, wave_count), f32),
            pltpu.VMEM((LANE, wave_count), f32),
            pltpu.VMEM((starts, wave_count), f32),
            pltpu.VMEM((starts, wave_count), f32),
            pltpu.VMEM((width, wave_count), b16),
            pltpu.VMEM((width, wave_count), b16),
            pltpu.VMEM((12 * rows, wave_count), b16),
            pltpu.VMEM((12 * rows, wave_count), b16),
            pltpu.VMEM((4 * rows, width), b16),
            pltpu.VMEM((4 * rows, width), b16),
            pltpu.VMEM((4, rows, width), f32),
        ],
        compiler_params=pltpu.CompilerParams(vmem_limit_bytes=40 * 1024 * 1024),
    )(row_points[None], scales, assignment[None, :], four)


def make_term(source, legendre):
    return jnp.einsum("knc,knt->ckt", source, legendre, preferred_element_type=jnp.float32)


def body(spectral, legendre, weights, points, assignment):
    own_slots, own_totals, column_count = spectral.shape
    wave_count = assignment.shape[0]
    levels = column_count // 8
    local_levels = levels // lax.axis_size("lev")
    own_waves = lax.dynamic_slice_in_dim(assignment, lax.axis_index("lat") * own_slots, own_slots)
    totals = lax.axis_index("lev") * own_totals + jnp.arange(own_totals, dtype=jnp.int32)
    triangle = totals[None, :] >= own_waves[:, None]
    masked = jnp.where(triangle[:, :, None], spectral, jnp.zeros((), spectral.dtype))
    summed = lax.psum_scatter(
        make_term(masked, legendre).astype(jnp.bfloat16), "lev", scatter_dimension=0, tiled=True
    )
    fourier = lax.all_to_all(summed, "lat", split_axis=2, concat_axis=1, tiled=True)
    pair_count = points.shape[0]
    grouped = fourier.reshape(local_levels, 2, 4, wave_count, pair_count, 2, 2)
    grouped = jnp.transpose(grouped, (4, 6, 1, 5, 0, 2, 3)).reshape(pair_count, 4, 8 * local_levels, wave_count)
    values, waves = [], []
    for pair in range(pair_count):
        scales = weights[2 * pair:2 * pair + 2] / points[pair].astype(jnp.float32)
        scales = jnp.repeat(scales, 4 * local_levels)[:, None]
        wave_rows, pair_values = grid_stage(grouped[pair], scales, points[pair], assignment)
        values.append(pair_values.reshape(2, local_levels, 4, NPAD))
        waves.append(wave_rows.reshape(2, 2, 2, local_levels, 4, wave_count))
    values = jnp.concatenate(values, axis=0)
    local_waves = jnp.transpose(jnp.stack(waves), (4, 1, 5, 6, 0, 3, 2))
    spread = lax.all_to_all(
        local_waves.reshape(8 * local_levels, wave_count, -1),
        "lat",
        split_axis=1,
        concat_axis=2,
        tiled=True,
    )
    result = jnp.einsum(
        "knt,ckt->knc",
        legendre,
        lax.all_gather(spread, "lev", axis=0, tiled=True),
        preferred_element_type=jnp.float32,
    )
    tendency = jnp.where(triangle[:, :, None], result, 0.0).astype(jnp.bfloat16)
    return (tendency, values)


def solution(mesh):
    in_specs = (P("lat", "lev", None), P("lat", "lev", None), P("lat"), P("lat"), P())
    out_specs = (P("lat", "lev", None), P("lat", "lev", None, None))
    return jax.shard_map(body, mesh=mesh, in_specs=in_specs, out_specs=out_specs, check_vma=False)
```

```python
import functools
import math

import jax
import jax.numpy as jnp
from jax import lax
from jax.experimental import pallas as pl
from jax.experimental.pallas import tpu as pltpu
from jax.sharding import PartitionSpec as P

NPAD = 5376
LANE = 128


def sincos(product, quarter, step):
    turns = jnp.floor(product * (1.0 / quarter) + 0.5)
    theta = (product - turns * quarter) * step
    square = theta * theta
    sine = theta * (1.0 + square * (-1.0 / 6 + square * (1.0 / 120 - square * (1.0 / 5040))))
    cosine = 1.0 + square * (-0.5 + square * (1.0 / 24 + square * (-1.0 / 720 + square * (1.0 / 40320))))
    quadrant = turns.astype(jnp.int32) & 3
    odd = (quadrant & 1) == 1
    first = jnp.where(odd, sine, cosine)
    second = jnp.where(odd, cosine, sine)
    return (
        jnp.where((quadrant == 1) | (quadrant == 2), -first, first),
        jnp.where(quadrant >= 2, -second, second),
    )


def shift_field(rows, shift):
    count = rows.shape[0]
    field = lax.broadcasted_iota(jnp.int32, rows.shape, 0) % 4
    return jnp.where(
        field < 4 - shift,
        pltpu.roll(rows, count - shift, axis=0),
        pltpu.roll(rows, 4 - shift, axis=0),
    )


def grid_kernel(
    points_ref, scales_ref, waves_ref, four_ref, out_ref, values_ref,
    base_cos, base_sin, start_cos, start_sin, cos_tab, sin_tab, lhs_cos, lhs_sin, term_cos, term_sin, images,
):
    width = cos_tab.shape[0]
    wave_count = cos_tab.shape[1]
    rows = four_ref.shape[1]
    blocks = width // LANE
    row_points = points_ref[0]
    quarter_int = row_points // 4
    quarter = quarter_int.astype(jnp.float32)
    step = (0.5 * math.pi) / quarter
    m_int = waves_ref[...]
    m_float = m_int.astype(jnp.float32)

    def start_rows(count, scale):
        return (lax.broadcasted_iota(jnp.int32, (count, 1), 0) * scale).astype(jnp.float32)

    start_cos[...], start_sin[...] = sincos(start_rows(start_cos.shape[0], LANE) * m_float, quarter, step)

    @pl.loop(0, LANE // 8)
    def _(index):
        at = pl.multiple_of(index * 8, 8)
        offsets = (lax.broadcasted_iota(jnp.int32, (8, 1), 0) + at).astype(jnp.float32)
        base_cos[pl.ds(at, 8), :], base_sin[pl.ds(at, 8), :] = sincos(offsets * m_float, quarter, step)

    @pl.loop(0, width // 16)
    def _(index):
        at = pl.multiple_of(index * 16, 16)
        low = pl.multiple_of((index % (LANE // 16)) * 16, 16)
        start = index // (LANE // 16)
        for col in range(0, wave_count, 2 * LANE):
            cols = pl.ds(col, 2 * LANE)
            bc = base_cos[pl.ds(low, 16), cols]
            bs = base_sin[pl.ds(low, 16), cols]
            sc = start_cos[pl.ds(start, 1), cols]
            ss = start_sin[pl.ds(start, 1), cols]
            cos_tab[pl.ds(at, 16), cols] = (sc * bc - ss * bs).astype(jnp.bfloat16)
            sin_tab[pl.ds(at, 16), cols] = (ss * bc + sc * bs).astype(jnp.bfloat16)

    active = 2 * m_int < row_points
    parity = jnp.where((m_int & 1) == 0, 1.0, -1.0)
    factor = jnp.where(active, jnp.where(m_int == 0, 1.0, 2.0), 0.0)
    slope = factor * (m_float * (1.0 / wave_count))
    part_rows = rows // 2

    def rows_of(slope_of, part):
        pieces = [four_ref[2 * row + slope_of].astype(jnp.float32) for row in range(2)]
        return jnp.concatenate([piece[part * part_rows:(part + 1) * part_rows] for piece in pieces], axis=0)

    real_value, imag_value, real_slope, imag_slope = rows_of(0, 0), rows_of(0, 1), rows_of(1, 0), rows_of(1, 1)

    def fill(lhs, value, zonal, merid):
        parts = [value, shift_field(value, 1), shift_field(value, 2), shift_field(value, 3), zonal, merid]
        for index, part in enumerate(parts):
            lhs[pl.ds(index * rows, rows), :] = part.astype(jnp.bfloat16)
            lhs[pl.ds((6 + index) * rows, rows), :] = (part * parity).astype(jnp.bfloat16)

    fill(lhs_cos, factor * real_value, -slope * imag_value, factor * real_slope)
    fill(lhs_sin, -factor * imag_value, -slope * real_value, -factor * imag_slope)
    scale = scales_ref[...]

    @pl.loop(0, blocks)
    def _(index):
        at = pl.multiple_of(index * LANE, LANE)
        contract = (((1,), (1,)), ((), ()))
        even = lax.dot_general(lhs_cos[...], cos_tab[pl.ds(at, LANE), :], contract, preferred_element_type=jnp.float32)
        odd = lax.dot_general(lhs_sin[...], sin_tab[pl.ds(at, LANE), :], contract, preferred_element_type=jnp.float32)
        place = lax.broadcasted_iota(jnp.int32, (1, LANE), 1) + at
        closed = place <= quarter_int
        inner = (place >= 1) & (place < quarter_int)
        half = 6 * rows
        fields = (
            (even[:half] + odd[:half], closed),
            (even[half:] + odd[half:], closed),
            (even[half:] - odd[half:], inner),
            (even[:half] - odd[:half], inner),
        )
        terms = []
        for image, (field, keep) in enumerate(fields):
            q0, q1, q2, q3, zonal, merid = (field[part * rows:(part + 1) * rows] for part in range(6))
            images[image, :, pl.ds(at, LANE)] = jnp.where(keep, q0, 0.0)
            weight = jnp.where(keep, scale, 0.0)
            terms.append(jnp.concatenate([(q1 * zonal + q2 * merid) * weight, q0 * q3 * weight], axis=0))
        cols = pl.ds(at, LANE)
        term_cos[:, cols] = jnp.concatenate([terms[0] + terms[3], terms[1] + terms[2]], axis=0).astype(jnp.bfloat16)
        term_sin[:, cols] = jnp.concatenate([terms[0] - terms[3], terms[1] - terms[2]], axis=0).astype(jnp.bfloat16)

    keep_wave = jnp.where(active, 1.0, 0.0)
    real = jnp.dot(term_cos[...], cos_tab[...], preferred_element_type=jnp.float32)
    imag = jnp.dot(term_sin[...], sin_tab[...], preferred_element_type=jnp.float32)
    split = 2 * rows
    real = (real[:split] + parity * real[split:]) * keep_wave
    imag = -(imag[:split] + parity * imag[split:]) * keep_wave
    for term in range(2):
        for row in range(2):
            low = term * rows + row * part_rows
            both = [real[low:low + part_rows], imag[low:low + part_rows]]
            out_ref[2 * row + term] = jnp.concatenate(both, axis=0).astype(out_ref.dtype)

    flip = (
        lax.broadcasted_iota(jnp.int32, (LANE, LANE), 0) + lax.broadcasted_iota(jnp.int32, (LANE, LANE), 1) == LANE - 1
    ).astype(jnp.float32).astype(jnp.bfloat16)
    pad = jnp.zeros((rows, NPAD - width), jnp.float32)

    def reverse(image):
        parts = [
            jnp.dot(images[image, :, pl.ds(block * LANE, LANE)].astype(jnp.bfloat16), flip, preferred_element_type=jnp.float32)
            for block in reversed(range(blocks))
        ]
        return jnp.concatenate(parts + [pad], axis=1)

    def straight(image):
        return jnp.concatenate([images[image], pad], axis=1)

    halfway = row_points // 2
    total = straight(0)
    total = total + pltpu.roll(straight(1), halfway, axis=1)
    total = total + pltpu.roll(reverse(2), lax.rem(halfway - (width - 1) + NPAD, NPAD), axis=1)
    total = total + pltpu.roll(reverse(3), lax.rem(row_points - (width - 1) + NPAD, NPAD), axis=1)
    values_ref[...] = total.astype(values_ref.dtype)


def grid_stage(four, scales, row_points, assignment):
    _, rows, wave_count = four.shape
    width = -(-(wave_count + 5) // LANE) * LANE
    starts = -(-(width // LANE) // 8) * 8
    smem, vmem = pl.BlockSpec(memory_space=pltpu.SMEM), pl.BlockSpec(memory_space=pltpu.VMEM)
    f32, b16 = jnp.float32, jnp.bfloat16
    return pl.pallas_call(
        grid_kernel,
        out_shape=(jax.ShapeDtypeStruct((4, rows, wave_count), b16), jax.ShapeDtypeStruct((rows, NPAD), b16)),
        in_specs=[smem, vmem, vmem, vmem],
        out_specs=(vmem, vmem),
        scratch_shapes=[
            pltpu.VMEM((LANE, wave_count), f32),
            pltpu.VMEM((LANE, wave_count), f32),
            pltpu.VMEM((starts, wave_count), f32),
            pltpu.VMEM((starts, wave_count), f32),
            pltpu.VMEM((width, wave_count), b16),
            pltpu.VMEM((width, wave_count), b16),
            pltpu.VMEM((12 * rows, wave_count), b16),
            pltpu.VMEM((12 * rows, wave_count), b16),
            pltpu.VMEM((4 * rows, width), b16),
            pltpu.VMEM((4 * rows, width), b16),
            pltpu.VMEM((4, rows, width), f32),
        ],
        compiler_params=pltpu.CompilerParams(vmem_limit_bytes=40 * 1024 * 1024),
    )(row_points[None], scales, assignment[None, :], four)


def split_column(column):
    return (column // 4 % 2) * 8 + column // 8 * 4 + column % 4


def greet(lat_size, lev_size):
    lat, lev = lax.axis_index("lat"), lax.axis_index("lev")
    barrier = pltpu.get_barrier_semaphore()
    for hop in range(1, lev_size):
        pl.semaphore_signal(barrier, inc=1, device_id=(lat, lax.rem(lev + hop, lev_size)), device_id_type=pl.DeviceIdType.MESH)
    for hop in range(1, lat_size):
        pl.semaphore_signal(barrier, inc=1, device_id=(lax.rem(lat + hop, lat_size), lev), device_id_type=pl.DeviceIdType.MESH)
    pl.semaphore_wait(barrier, lat_size + lev_size - 2)


def remote(src, dst, send_sem, recv_sem, device):
    return pltpu.make_async_remote_copy(
        src_ref=src, dst_ref=dst, send_sem=send_sem, recv_sem=recv_sem,
        device_id=device, device_id_type=pl.DeviceIdType.MESH,
    )


def inverse_kernel(
    lat_size, lev_size, pack, chunks,
    own_ref, spec_hbm, leg_hbm, out_ref,
    spec, leg, lev_send, lev_recv, summed, turned, lat_send, lat_recv,
    load_sem, lev_send_sem, lev_recv_sem, lat_send_sem, lat_recv_sem,
):
    lat, lev = lax.axis_index("lat"), lax.axis_index("lev")
    _, groups, columns, totals = spec.shape
    rows = leg.shape[2]
    size = groups // chunks
    loads = []
    for chunk in range(chunks):
        part = pl.ds(chunk * size, size)
        pair = [
            pltpu.make_async_copy(spec_hbm.at[:, part], spec.at[:, part], load_sem.at[chunk, 0]),
            pltpu.make_async_copy(leg_hbm.at[:, part], leg.at[:, part], load_sem.at[chunk, 1]),
        ]
        for copy in pair:
            copy.start()
        loads.append(pair)
    greet(lat_size, lev_size)
    number = lax.broadcasted_iota(jnp.int32, (1, totals), 1) + lev * totals
    lane = lax.broadcasted_iota(jnp.int32, (1, pack * rows), 1) // rows
    share = columns // lev_size
    copies = []
    for chunk in range(chunks):
        for copy in loads[chunk]:
            copy.wait()

        @pl.loop(chunk * size, (chunk + 1) * size)
        def _(group):
            tables = []
            for which in range(pack):
                kept = jnp.where(number >= own_ref[which * groups + group], 1.0, 0.0).astype(jnp.bfloat16)
                tables.append(leg[which, group] * kept)
            table = jnp.concatenate(tables, axis=0)
            source = jnp.concatenate([spec[which, group] for which in range(pack)], axis=0)
            product = lax.dot_general(source, table, (((1,), (1,)), ((), ())), preferred_element_type=jnp.float32)
            result = product[:columns]
            for which in range(1, pack):
                result = jnp.where(lane == which, product[which * columns:(which + 1) * columns], result)
            result = result.astype(jnp.bfloat16)
            for peer in range(lev_size):
                lev_send[peer, group] = result[peer * share:(peer + 1) * share]

        part = pl.ds(chunk * size, size)
        for hop in range(1, lev_size):
            peer = lax.rem(lev + hop, lev_size)
            copy = remote(
                lev_send.at[peer, part], lev_recv.at[hop - 1, part],
                lev_send_sem.at[chunk, hop - 1], lev_recv_sem.at[chunk, hop - 1], (lat, peer),
            )
            copy.start()
            copies.append(copy)
    for chunk in range(chunks):
        for hop in range(1, lev_size):
            copies[chunk * (lev_size - 1) + hop - 1].wait_recv()
        part = pl.ds(chunk * size, size)
        total = lev_send[lev, part].astype(jnp.float32)
        for hop in range(1, lev_size):
            total = total + lev_recv[hop - 1, part].astype(jnp.float32)
        summed[part] = total
    for column in range(share):
        flat = jnp.transpose(summed[:, column, :])
        turned[:, split_column(column), :] = jnp.concatenate(
            [flat[which * rows:(which + 1) * rows] for which in range(pack)], axis=1
        )
    lat_send[...] = turned[...].astype(jnp.bfloat16)
    block = rows // lat_size
    swaps = []
    for hop in range(1, lat_size):
        peer = lax.rem(lat + hop, lat_size)
        copy = remote(
            lat_send.at[pl.ds(peer * block, block)], lat_recv.at[lat],
            lat_send_sem.at[hop - 1], lat_recv_sem.at[hop - 1], (peer, lev),
        )
        copy.start()
        swaps.append(copy)
    lat_recv[lat] = lat_send[pl.ds(lat * block, block)]
    for copy in copies:
        copy.wait_send()
    for copy in swaps:
        copy.wait()
    for row in range(block):
        pieces = [lat_recv[source, row].astype(jnp.float32) for source in range(lat_size)]
        out_ref[row] = jnp.concatenate(pieces, axis=1).astype(jnp.bfloat16)


def direct_kernel(
    lat_size, lev_size, pack,
    waves_ref, out_ref,
    lat_send, lat_recv, turned, grouped, lev_send, lev_recv,
    lat_send_sem, lat_recv_sem, lev_send_sem, lev_recv_sem,
):
    lat, lev = lax.axis_index("lat"), lax.axis_index("lev")
    block, share, _ = waves_ref.shape
    own = lat_send.shape[3]
    rows, groups = lat_size * block, own // pack
    for row in range(block):
        line = waves_ref[row].astype(jnp.float32)
        for peer in range(lat_size):
            lat_send[peer, row] = line[:, peer * own:(peer + 1) * own].astype(jnp.bfloat16)
    greet(lat_size, lev_size)
    swaps = []
    for hop in range(1, lat_size):
        peer = lax.rem(lat + hop, lat_size)
        copy = remote(lat_send.at[peer], lat_recv.at[lat], lat_send_sem.at[hop - 1], lat_recv_sem.at[hop - 1], (peer, lev))
        copy.start()
        swaps.append(copy)
    lat_recv[lat] = lat_send[lat]
    for copy in swaps:
        copy.wait()
    turned[...] = lat_recv[...].astype(jnp.float32).reshape(rows, share, own)
    for column in range(share):
        line = turned[:, split_column(column), :]
        flat = jnp.concatenate([line[:, which * groups:(which + 1) * groups] for which in range(pack)], axis=0)
        grouped[:, column, :] = jnp.transpose(flat)
    lev_send[...] = grouped[...].astype(jnp.bfloat16)
    copies = []
    for hop in range(1, lev_size):
        peer = lax.rem(lev + hop, lev_size)
        copy = remote(lev_send, lev_recv.at[lev], lev_send_sem.at[hop - 1], lev_recv_sem.at[hop - 1], (lat, peer))
        copy.start()
        copies.append(copy)
    lev_recv[lev] = lev_send[...]
    for copy in copies:
        copy.wait()
    out_ref[...] = lev_recv[...]


def tendency_kernel(own_ref, waves_ref, leg_ref, out_ref):
    pack, size, rows, totals = leg_ref.shape
    groups = size * pl.num_programs(0)
    lev_size, _, share, lanes = waves_ref.shape
    columns = lev_size * share
    first = pl.program_id(0) * size
    number = lax.broadcasted_iota(jnp.int32, (1, totals), 1) + lax.axis_index("lev") * totals
    lane = lax.broadcasted_iota(jnp.int32, (1, lanes), 1) // rows

    @pl.loop(0, size)
    def _(group):
        waves = jnp.concatenate([waves_ref[peer, group] for peer in range(lev_size)], axis=0)
        spread = jnp.concatenate(
            [waves * jnp.where(lane == which, 1.0, 0.0).astype(jnp.bfloat16) for which in range(pack)], axis=0
        )
        table = jnp.concatenate([leg_ref[which, group] for which in range(pack)], axis=0)
        product = jnp.dot(spread, table, preferred_element_type=jnp.float32)
        for which in range(pack):
            kept = number >= own_ref[which * groups + first + group]
            out_ref[which, group] = jnp.where(kept, product[which * columns:(which + 1) * columns], 0.0).astype(jnp.bfloat16)


def body(spectral, legendre, weights, points, assignment):
    own_slots, own_totals, column_count = spectral.shape
    wave_count = assignment.shape[0]
    rows = legendre.shape[2]
    levels = column_count // 8
    lat_size, lev_size = lax.axis_size("lat"), lax.axis_size("lev")
    local_levels = levels // lev_size
    share = column_count // lev_size
    pack = LANE // rows
    groups = own_slots // pack
    block = rows // lat_size
    chunks = 5
    own_waves = lax.dynamic_slice_in_dim(assignment, lax.axis_index("lat") * own_slots, own_slots)
    spec_in = jnp.transpose(spectral, (0, 2, 1)).reshape(pack, groups, column_count, own_totals)
    leg_in = jnp.transpose(legendre, (0, 2, 1)).reshape(pack, groups, rows, own_totals)
    smem, vmem = pl.BlockSpec(memory_space=pltpu.SMEM), pl.BlockSpec(memory_space=pltpu.VMEM)
    anywhere = pl.BlockSpec(memory_space=pl.ANY)
    f32, b16 = jnp.float32, jnp.bfloat16
    dma = pltpu.SemaphoreType.DMA
    fourier = pl.pallas_call(
        functools.partial(inverse_kernel, lat_size, lev_size, pack, chunks),
        out_shape=jax.ShapeDtypeStruct((block, share, wave_count), b16),
        in_specs=[smem, anywhere, anywhere],
        out_specs=vmem,
        scratch_shapes=[
            pltpu.VMEM((pack, groups, column_count, own_totals), b16),
            pltpu.VMEM((pack, groups, rows, own_totals), b16),
            pltpu.VMEM((lev_size, groups, share, pack * rows), b16),
            pltpu.VMEM((lev_size - 1, groups, share, pack * rows), b16),
            pltpu.VMEM((groups, share, pack * rows), f32),
            pltpu.VMEM((rows, share, own_slots), f32),
            pltpu.VMEM((rows, share, own_slots), b16),
            pltpu.VMEM((lat_size, block, share, own_slots), b16),
            dma((chunks, 2)), dma((chunks, lev_size - 1)), dma((chunks, lev_size - 1)),
            dma((lat_size - 1,)), dma((lat_size - 1,)),
        ],
        compiler_params=pltpu.CompilerParams(
            collective_id=0, has_side_effects=True, vmem_limit_bytes=40 * 1024 * 1024
        ),
    )(own_waves, spec_in, leg_in)
    scales = weights / points[0].astype(jnp.float32)
    scales = jnp.repeat(scales, 4 * local_levels)[:, None]
    wave_rows, values = grid_stage(fourier, scales, points[0], assignment)
    values = values.reshape(2, local_levels, 4, NPAD)
    gathered = pl.pallas_call(
        functools.partial(direct_kernel, lat_size, lev_size, pack),
        out_shape=jax.ShapeDtypeStruct((lev_size, groups, share, pack * rows), b16),
        in_specs=[vmem],
        out_specs=vmem,
        scratch_shapes=[
            pltpu.VMEM((lat_size, block, share, own_slots), b16),
            pltpu.VMEM((lat_size, block, share, own_slots), b16),
            pltpu.VMEM((rows, share, own_slots), f32),
            pltpu.VMEM((groups, share, pack * rows), f32),
            pltpu.VMEM((groups, share, pack * rows), b16),
            pltpu.VMEM((lev_size, groups, share, pack * rows), b16),
            dma((lat_size - 1,)), dma((lat_size - 1,)), dma((lev_size - 1,)), dma((lev_size - 1,)),
        ],
        compiler_params=pltpu.CompilerParams(
            collective_id=1, has_side_effects=True, vmem_limit_bytes=40 * 1024 * 1024
        ),
    )(wave_rows)
    size = groups // 5
    result = pl.pallas_call(
        tendency_kernel,
        grid=(groups // size,),
        out_shape=jax.ShapeDtypeStruct((pack, groups, column_count, own_totals), b16),
        in_specs=[
            smem,
            pl.BlockSpec((lev_size, size, share, pack * rows), lambda step: (0, step, 0, 0)),
            pl.BlockSpec((pack, size, rows, own_totals), lambda step: (0, step, 0, 0)),
        ],
        out_specs=pl.BlockSpec((pack, size, column_count, own_totals), lambda step: (0, step, 0, 0)),
        compiler_params=pltpu.CompilerParams(vmem_limit_bytes=40 * 1024 * 1024),
    )(own_waves, gathered, leg_in)
    tendency = jnp.transpose(result.reshape(own_slots, column_count, own_totals), (0, 2, 1))
    return (tendency, values)


def solution(mesh):
    in_specs = (P("lat", "lev", None), P("lat", "lev", None), P("lat"), P("lat"), P())
    out_specs = (P("lat", "lev", None), P("lat", "lev", None, None))
    return jax.shard_map(body, mesh=mesh, in_specs=in_specs, out_specs=out_specs, check_vma=False)
```

```python
import functools
import math

import jax
import jax.numpy as jnp
from jax import lax
from jax.experimental import pallas as pl
from jax.experimental.pallas import tpu as pltpu
from jax.sharding import PartitionSpec as P

NPAD = 5376
LANE = 128


def sincos(product, quarter, step):
    turns = jnp.floor(product * (1.0 / quarter) + 0.5)
    theta = (product - turns * quarter) * step
    square = theta * theta
    sine = theta * (1.0 + square * (-1.0 / 6 + square * (1.0 / 120 - square * (1.0 / 5040))))
    cosine = 1.0 + square * (-0.5 + square * (1.0 / 24 + square * (-1.0 / 720 + square * (1.0 / 40320))))
    quadrant = turns.astype(jnp.int32) & 3
    odd = (quadrant & 1) == 1
    first = jnp.where(odd, sine, cosine)
    second = jnp.where(odd, cosine, sine)
    return (
        jnp.where((quadrant == 1) | (quadrant == 2), -first, first),
        jnp.where(quadrant >= 2, -second, second),
    )


def shift_field(rows, shift):
    count = rows.shape[0]
    field = lax.broadcasted_iota(jnp.int32, rows.shape, 0) % 4
    return jnp.where(
        field < 4 - shift,
        pltpu.roll(rows, count - shift, axis=0),
        pltpu.roll(rows, 4 - shift, axis=0),
    )


def build_tables(points_ref, waves_ref, base_cos, base_sin, start_cos, start_sin, cos_tab, sin_tab):
    width = cos_tab.shape[0]
    wave_count = cos_tab.shape[1]
    row_points = points_ref[0]
    quarter_int = row_points // 4
    quarter = quarter_int.astype(jnp.float32)
    step = (0.5 * math.pi) / quarter
    m_int = waves_ref[...]
    m_float = m_int.astype(jnp.float32)

    def start_rows(count, scale):
        return (lax.broadcasted_iota(jnp.int32, (count, 1), 0) * scale).astype(jnp.float32)

    start_cos[...], start_sin[...] = sincos(start_rows(start_cos.shape[0], LANE) * m_float, quarter, step)

    @pl.loop(0, LANE // 8, unroll=2)
    def _(index):
        at = pl.multiple_of(index * 8, 8)
        offsets = (lax.broadcasted_iota(jnp.int32, (8, 1), 0) + at).astype(jnp.float32)
        base_cos[pl.ds(at, 8), :], base_sin[pl.ds(at, 8), :] = sincos(offsets * m_float, quarter, step)

    @pl.loop(0, width // 16, unroll=2)
    def _(index):
        at = pl.multiple_of(index * 16, 16)
        low = pl.multiple_of((index % (LANE // 16)) * 16, 16)
        start = index // (LANE // 16)
        for col in range(0, wave_count, 2 * LANE):
            cols = pl.ds(col, 2 * LANE)
            bc = base_cos[pl.ds(low, 16), cols]
            bs = base_sin[pl.ds(low, 16), cols]
            sc = start_cos[pl.ds(start, 1), cols]
            ss = start_sin[pl.ds(start, 1), cols]
            cos_tab[pl.ds(at, 16), cols] = (sc * bc - ss * bs).astype(jnp.bfloat16)
            sin_tab[pl.ds(at, 16), cols] = (ss * bc + sc * bs).astype(jnp.bfloat16)


def grid_rows(
    points_ref, scales_ref, waves_ref, four_ref, out_ref,
    cos_tab, sin_tab, lhs_cos, lhs_sin, term_cos, term_sin, images,
):
    width, wave_count = cos_tab.shape
    rows = four_ref.shape[1]
    blocks = width // LANE
    row_points = points_ref[0]
    quarter_int = row_points // 4
    m_int = waves_ref[...]
    m_float = m_int.astype(jnp.float32)
    active = 2 * m_int < row_points
    parity = jnp.where((m_int & 1) == 0, 1.0, -1.0)
    factor = jnp.where(active, jnp.where(m_int == 0, 1.0, 2.0), 0.0)
    slope = factor * (m_float * (1.0 / wave_count))
    part_rows = rows // 2

    def rows_of(slope_of, part):
        pieces = [four_ref[2 * row + slope_of].astype(jnp.float32) for row in range(2)]
        return jnp.concatenate([piece[part * part_rows:(part + 1) * part_rows] for piece in pieces], axis=0)

    real_value, imag_value, real_slope, imag_slope = rows_of(0, 0), rows_of(0, 1), rows_of(1, 0), rows_of(1, 1)

    def fill(lhs, value, zonal, merid):
        parts = [value, shift_field(value, 1), shift_field(value, 2), shift_field(value, 3), zonal, merid]
        for index, part in enumerate(parts):
            lhs[pl.ds(index * rows, rows), :] = part.astype(jnp.bfloat16)
            lhs[pl.ds((6 + index) * rows, rows), :] = (part * parity).astype(jnp.bfloat16)

    fill(lhs_cos, factor * real_value, -slope * imag_value, factor * real_slope)
    fill(lhs_sin, -factor * imag_value, -slope * real_value, -factor * imag_slope)
    scale = scales_ref[...]

    for index in range(blocks):
        at = index * LANE
        contract = (((1,), (1,)), ((), ()))
        even = lax.dot_general(lhs_cos[...], cos_tab[pl.ds(at, LANE), :], contract, preferred_element_type=jnp.float32)
        odd = lax.dot_general(lhs_sin[...], sin_tab[pl.ds(at, LANE), :], contract, preferred_element_type=jnp.float32)
        place = lax.broadcasted_iota(jnp.int32, (1, LANE), 1) + at
        closed = place <= quarter_int
        inner = (place >= 1) & (place < quarter_int)
        half = 6 * rows
        fields = (
            (even[:half] + odd[:half], closed),
            (even[half:] + odd[half:], closed),
            (even[half:] - odd[half:], inner),
            (even[:half] - odd[:half], inner),
        )
        terms = []
        for image, (field, keep) in enumerate(fields):
            q0, q1, q2, q3, zonal, merid = (field[part * rows:(part + 1) * rows] for part in range(6))
            images[image, :, pl.ds(at, LANE)] = jnp.where(keep, q0, 0.0)
            weight = jnp.where(keep, scale, 0.0)
            terms.append(jnp.concatenate([(q1 * zonal + q2 * merid) * weight, q0 * q3 * weight], axis=0))
        cols = pl.ds(at, LANE)
        term_cos[:, cols] = jnp.concatenate([terms[0] + terms[3], terms[1] + terms[2]], axis=0).astype(jnp.bfloat16)
        term_sin[:, cols] = jnp.concatenate([terms[0] - terms[3], terms[1] - terms[2]], axis=0).astype(jnp.bfloat16)

    keep_wave = jnp.where(active, 1.0, 0.0)
    real = jnp.dot(term_cos[...], cos_tab[...], preferred_element_type=jnp.float32)
    imag = jnp.dot(term_sin[...], sin_tab[...], preferred_element_type=jnp.float32)
    split = 2 * rows
    real = (real[:split] + parity * real[split:]) * keep_wave
    imag = -(imag[:split] + parity * imag[split:]) * keep_wave
    for term in range(2):
        for row in range(2):
            low = term * rows + row * part_rows
            both = [real[low:low + part_rows], imag[low:low + part_rows]]
            out_ref[2 * row + term] = jnp.concatenate(both, axis=0).astype(out_ref.dtype)


def place_values(points_ref, images, values_ref):
    _, rows, width = images.shape
    blocks = width // LANE
    row_points = points_ref[0]
    flip = (
        lax.broadcasted_iota(jnp.int32, (LANE, LANE), 0) + lax.broadcasted_iota(jnp.int32, (LANE, LANE), 1) == LANE - 1
    ).astype(jnp.float32).astype(jnp.bfloat16)
    pad = jnp.zeros((rows, NPAD - width), jnp.float32)

    def reverse(image):
        parts = [
            jnp.dot(images[image, :, pl.ds(block * LANE, LANE)].astype(jnp.bfloat16), flip, preferred_element_type=jnp.float32)
            for block in reversed(range(blocks))
        ]
        return jnp.concatenate(parts + [pad], axis=1)

    def straight(image):
        return jnp.concatenate([images[image], pad], axis=1)

    halfway = row_points // 2
    total = straight(0)
    total = total + pltpu.roll(straight(1), halfway, axis=1)
    total = total + pltpu.roll(reverse(2), lax.rem(halfway - (width - 1) + NPAD, NPAD), axis=1)
    total = total + pltpu.roll(reverse(3), lax.rem(row_points - (width - 1) + NPAD, NPAD), axis=1)
    values_ref[...] = total.astype(values_ref.dtype)


def split_column(column):
    return (column // 4 % 2) * 8 + column // 8 * 4 + column % 4


def greet(lat_size, lev_size):
    lat, lev = lax.axis_index("lat"), lax.axis_index("lev")
    barrier = pltpu.get_barrier_semaphore()
    for hop in range(1, lev_size):
        pl.semaphore_signal(barrier, inc=1, device_id=(lat, lax.rem(lev + hop, lev_size)), device_id_type=pl.DeviceIdType.MESH)
    for hop in range(1, lat_size):
        pl.semaphore_signal(barrier, inc=1, device_id=(lax.rem(lat + hop, lat_size), lev), device_id_type=pl.DeviceIdType.MESH)
    pl.semaphore_wait(barrier, lat_size + lev_size - 2)


def remote(src, dst, send_sem, recv_sem, device):
    return pltpu.make_async_remote_copy(
        src_ref=src, dst_ref=dst, send_sem=send_sem, recv_sem=recv_sem,
        device_id=device, device_id_type=pl.DeviceIdType.MESH,
    )


def transform_kernel(
    lat_size, lev_size, pack, chunks,
    own_ref, points_ref, scales_ref, waves_ref, spec_hbm, leg_hbm, out_ref, images,
    spec, leg, lev_send, lev_recv, summed, turned, lat_send, lat_recv,
    load_sem, lev_send_sem, lev_recv_sem, lat_send_sem, lat_recv_sem,
    four, wave_rows, base_cos, base_sin, start_cos, start_sin, cos_tab, sin_tab,
    lhs_cos, lhs_sin, term_cos, term_sin,
    back_send, back_recv, back_turned, grouped, all_send, all_recv,
    back_send_sem, back_recv_sem, all_send_sem, all_recv_sem,
):
    lat, lev = lax.axis_index("lat"), lax.axis_index("lev")
    _, groups, columns, totals = spec.shape
    rows = leg.shape[2]
    size = groups // chunks
    loads = []
    for chunk in range(chunks):
        part = pl.ds(chunk * size, size)
        pair = [
            pltpu.make_async_copy(spec_hbm.at[:, part], spec.at[:, part], load_sem.at[chunk, 0]),
            pltpu.make_async_copy(leg_hbm.at[:, part], leg.at[:, part], load_sem.at[chunk, 1]),
        ]
        for copy in pair:
            copy.start()
        loads.append(pair)
    greet(lat_size, lev_size)
    number = lax.broadcasted_iota(jnp.int32, (1, totals), 1) + lev * totals
    lane = lax.broadcasted_iota(jnp.int32, (1, pack * rows), 1) // rows
    share = columns // lev_size
    copies = []
    for chunk in range(chunks):
        for copy in loads[chunk]:
            copy.wait()

        @pl.loop(chunk * size, (chunk + 1) * size, unroll=4)
        def _(group):
            tables = []
            for which in range(pack):
                kept = jnp.where(number >= own_ref[which * groups + group], 1.0, 0.0).astype(jnp.bfloat16)
                tables.append(leg[which, group] * kept)
            table = jnp.concatenate(tables, axis=0)
            source = jnp.concatenate([spec[which, group] for which in range(pack)], axis=0)
            product = lax.dot_general(source, table, (((1,), (1,)), ((), ())), preferred_element_type=jnp.float32)
            result = product[:columns]
            for which in range(1, pack):
                result = jnp.where(lane == which, product[which * columns:(which + 1) * columns], result)
            result = result.astype(jnp.bfloat16)
            for peer in range(lev_size):
                lev_send[peer, group] = result[peer * share:(peer + 1) * share]

        part = pl.ds(chunk * size, size)
        for hop in range(1, lev_size):
            peer = lax.rem(lev + hop, lev_size)
            copy = remote(
                lev_send.at[peer, part], lev_recv.at[hop - 1, part],
                lev_send_sem.at[chunk, hop - 1], lev_recv_sem.at[chunk, hop - 1], (lat, peer),
            )
            copy.start()
            copies.append(copy)
    build_tables(points_ref, waves_ref, base_cos, base_sin, start_cos, start_sin, cos_tab, sin_tab)
    for chunk in range(chunks):
        for hop in range(1, lev_size):
            copies[chunk * (lev_size - 1) + hop - 1].wait_recv()
        part = pl.ds(chunk * size, size)
        total = lev_send[lev, part].astype(jnp.float32)
        for hop in range(1, lev_size):
            total = total + lev_recv[hop - 1, part].astype(jnp.float32)
        summed[part] = total
    for column in range(share):
        flat = jnp.transpose(summed[:, column, :])
        turned[:, split_column(column), :] = jnp.concatenate(
            [flat[which * rows:(which + 1) * rows] for which in range(pack)], axis=1
        )
    lat_send[...] = turned[...].astype(jnp.bfloat16)
    block = rows // lat_size
    swaps = []
    for hop in range(1, lat_size):
        peer = lax.rem(lat + hop, lat_size)
        copy = remote(
            lat_send.at[pl.ds(peer * block, block)], lat_recv.at[lat],
            lat_send_sem.at[hop - 1], lat_recv_sem.at[hop - 1], (peer, lev),
        )
        copy.start()
        swaps.append(copy)
    lat_recv[lat] = lat_send[pl.ds(lat * block, block)]
    for copy in copies:
        copy.wait_send()
    for copy in swaps:
        copy.wait()
    for row in range(block):
        pieces = [lat_recv[source, row].astype(jnp.float32) for source in range(lat_size)]
        four[row] = jnp.concatenate(pieces, axis=1).astype(jnp.bfloat16)
    grid_rows(
        points_ref, scales_ref, waves_ref, four, wave_rows,
        cos_tab, sin_tab, lhs_cos, lhs_sin, term_cos, term_sin, images,
    )
    direct_steps(
        lat_size, lev_size, pack, wave_rows, out_ref,
        back_send, back_recv, back_turned, grouped, all_send, all_recv,
        back_send_sem, back_recv_sem, all_send_sem, all_recv_sem,
    )


def direct_steps(
    lat_size, lev_size, pack,
    waves_ref, out_ref,
    lat_send, lat_recv, turned, grouped, lev_send, lev_recv,
    lat_send_sem, lat_recv_sem, lev_send_sem, lev_recv_sem,
):
    lat, lev = lax.axis_index("lat"), lax.axis_index("lev")
    block, share, _ = waves_ref.shape
    own = lat_send.shape[3]
    rows, groups = lat_size * block, own // pack
    for row in range(block):
        line = waves_ref[row].astype(jnp.float32)
        for peer in range(lat_size):
            lat_send[peer, row] = line[:, peer * own:(peer + 1) * own].astype(jnp.bfloat16)
    swaps = []
    for hop in range(1, lat_size):
        peer = lax.rem(lat + hop, lat_size)
        copy = remote(lat_send.at[peer], lat_recv.at[lat], lat_send_sem.at[hop - 1], lat_recv_sem.at[hop - 1], (peer, lev))
        copy.start()
        swaps.append(copy)
    lat_recv[lat] = lat_send[lat]
    for copy in swaps:
        copy.wait()
    turned[...] = lat_recv[...].astype(jnp.float32).reshape(rows, share, own)
    for column in range(share):
        line = turned[:, split_column(column), :]
        flat = jnp.concatenate([line[:, which * groups:(which + 1) * groups] for which in range(pack)], axis=0)
        grouped[:, column, :] = jnp.transpose(flat)
    lev_send[...] = grouped[...].astype(jnp.bfloat16)
    copies = []
    for hop in range(1, lev_size):
        peer = lax.rem(lev + hop, lev_size)
        copy = remote(lev_send, lev_recv.at[lev], lev_send_sem.at[hop - 1], lev_recv_sem.at[hop - 1], (lat, peer))
        copy.start()
        copies.append(copy)
    lev_recv[lev] = lev_send[...]
    for copy in copies:
        copy.wait()
    out_ref[...] = lev_recv[...]


def tendency_kernel(own_ref, points_ref, waves_ref, leg_ref, images, out_ref, values_ref):
    pack, size, rows, totals = leg_ref.shape
    groups = size * pl.num_programs(0)
    lev_size, _, share, lanes = waves_ref.shape
    columns = lev_size * share
    first = pl.program_id(0) * size
    number = lax.broadcasted_iota(jnp.int32, (1, totals), 1) + lax.axis_index("lev") * totals
    lane = lax.broadcasted_iota(jnp.int32, (1, lanes), 1) // rows

    @pl.when(pl.program_id(0) == 0)
    def _():
        place_values(points_ref, images, values_ref)

    @pl.loop(0, size, unroll=4)
    def _(group):
        waves = jnp.concatenate([waves_ref[peer, group] for peer in range(lev_size)], axis=0)
        spread = jnp.concatenate(
            [waves * jnp.where(lane == which, 1.0, 0.0).astype(jnp.bfloat16) for which in range(pack)], axis=0
        )
        table = jnp.concatenate([leg_ref[which, group] for which in range(pack)], axis=0)
        product = jnp.dot(spread, table, preferred_element_type=jnp.float32)
        for which in range(pack):
            kept = number >= own_ref[which * groups + first + group]
            out_ref[which, group] = jnp.where(kept, product[which * columns:(which + 1) * columns], 0.0).astype(jnp.bfloat16)


def body(spectral, legendre, weights, points, assignment):
    own_slots, own_totals, column_count = spectral.shape
    wave_count = assignment.shape[0]
    rows = legendre.shape[2]
    levels = column_count // 8
    lat_size, lev_size = lax.axis_size("lat"), lax.axis_size("lev")
    local_levels = levels // lev_size
    share = column_count // lev_size
    pack = LANE // rows
    groups = own_slots // pack
    block = rows // lat_size
    chunks = 5
    own_waves = lax.dynamic_slice_in_dim(assignment, lax.axis_index("lat") * own_slots, own_slots)
    spec_in = jnp.transpose(spectral, (0, 2, 1)).reshape(pack, groups, column_count, own_totals)
    leg_in = jnp.transpose(legendre, (0, 2, 1)).reshape(pack, groups, rows, own_totals)
    smem, vmem = pl.BlockSpec(memory_space=pltpu.SMEM), pl.BlockSpec(memory_space=pltpu.VMEM)
    anywhere = pl.BlockSpec(memory_space=pl.ANY)
    f32, b16 = jnp.float32, jnp.bfloat16
    dma = pltpu.SemaphoreType.DMA
    width = -(-(wave_count + 5) // LANE) * LANE
    starts = -(-(width // LANE) // 8) * 8
    scales = weights / points[0].astype(f32)
    scales = jnp.repeat(scales, 4 * local_levels)[:, None]
    gathered, images = pl.pallas_call(
        functools.partial(transform_kernel, lat_size, lev_size, pack, chunks),
        out_shape=(
            jax.ShapeDtypeStruct((lev_size, groups, share, pack * rows), b16),
            jax.ShapeDtypeStruct((4, share, width), f32),
        ),
        in_specs=[smem, smem, vmem, vmem, anywhere, anywhere],
        out_specs=(vmem, vmem),
        scratch_shapes=[
            pltpu.VMEM((pack, groups, column_count, own_totals), b16),
            pltpu.VMEM((pack, groups, rows, own_totals), b16),
            pltpu.VMEM((lev_size, groups, share, pack * rows), b16),
            pltpu.VMEM((lev_size - 1, groups, share, pack * rows), b16),
            pltpu.VMEM((groups, share, pack * rows), f32),
            pltpu.VMEM((rows, share, own_slots), f32),
            pltpu.VMEM((rows, share, own_slots), b16),
            pltpu.VMEM((lat_size, block, share, own_slots), b16),
            dma((chunks, 2)), dma((chunks, lev_size - 1)), dma((chunks, lev_size - 1)),
            dma((lat_size - 1,)), dma((lat_size - 1,)),
            pltpu.VMEM((block, share, wave_count), b16),
            pltpu.VMEM((block, share, wave_count), b16),
            pltpu.VMEM((LANE, wave_count), f32),
            pltpu.VMEM((LANE, wave_count), f32),
            pltpu.VMEM((starts, wave_count), f32),
            pltpu.VMEM((starts, wave_count), f32),
            pltpu.VMEM((width, wave_count), b16),
            pltpu.VMEM((width, wave_count), b16),
            pltpu.VMEM((12 * share, wave_count), b16),
            pltpu.VMEM((12 * share, wave_count), b16),
            pltpu.VMEM((4 * share, width), b16),
            pltpu.VMEM((4 * share, width), b16),
            pltpu.VMEM((lat_size, block, share, own_slots), b16),
            pltpu.VMEM((lat_size, block, share, own_slots), b16),
            pltpu.VMEM((rows, share, own_slots), f32),
            pltpu.VMEM((groups, share, pack * rows), f32),
            pltpu.VMEM((groups, share, pack * rows), b16),
            pltpu.VMEM((lev_size, groups, share, pack * rows), b16),
            dma((lat_size - 1,)), dma((lat_size - 1,)), dma((lev_size - 1,)), dma((lev_size - 1,)),
        ],
        compiler_params=pltpu.CompilerParams(
            collective_id=0, has_side_effects=True, vmem_limit_bytes=60 * 1024 * 1024
        ),
    )(own_waves, points, scales, assignment[None, :], spec_in, leg_in)
    size = groups // 5
    result, values = pl.pallas_call(
        tendency_kernel,
        grid=(groups // size,),
        out_shape=(
            jax.ShapeDtypeStruct((pack, groups, column_count, own_totals), b16),
            jax.ShapeDtypeStruct((share, NPAD), b16),
        ),
        in_specs=[
            smem,
            smem,
            pl.BlockSpec((lev_size, size, share, pack * rows), lambda step: (0, step, 0, 0)),
            pl.BlockSpec((pack, size, rows, own_totals), lambda step: (0, step, 0, 0)),
            vmem,
        ],
        out_specs=(
            pl.BlockSpec((pack, size, column_count, own_totals), lambda step: (0, step, 0, 0)),
            vmem,
        ),
        compiler_params=pltpu.CompilerParams(vmem_limit_bytes=60 * 1024 * 1024),
    )(own_waves, points, gathered, leg_in, images)
    values = values.reshape(2, local_levels, 4, NPAD)
    tendency = jnp.transpose(result.reshape(own_slots, column_count, own_totals), (0, 2, 1))
    return (tendency, values)


def solution(mesh):
    in_specs = (P("lat", "lev", None), P("lat", "lev", None), P("lat"), P("lat"), P())
    out_specs = (P("lat", "lev", None), P("lat", "lev", None, None))
    return jax.shard_map(body, mesh=mesh, in_specs=in_specs, out_specs=out_specs, check_vma=False)
```

```python
import functools
import math

import jax
import jax.numpy as jnp
from jax import lax
from jax.experimental import pallas as pl
from jax.experimental.pallas import tpu as pltpu
from jax.sharding import PartitionSpec as P

NPAD = 5376
LANE = 128


def sincos(product, quarter, step):
    turns = jnp.floor(product * (1.0 / quarter) + 0.5)
    theta = (product - turns * quarter) * step
    square = theta * theta
    sine = theta * (1.0 + square * (-1.0 / 6 + square * (1.0 / 120 - square * (1.0 / 5040))))
    cosine = 1.0 + square * (-0.5 + square * (1.0 / 24 + square * (-1.0 / 720 + square * (1.0 / 40320))))
    quadrant = turns.astype(jnp.int32) & 3
    odd = (quadrant & 1) == 1
    first = jnp.where(odd, sine, cosine)
    second = jnp.where(odd, cosine, sine)
    return (
        jnp.where((quadrant == 1) | (quadrant == 2), -first, first),
        jnp.where(quadrant >= 2, -second, second),
    )


def shift_field(rows, shift):
    count = rows.shape[0]
    field = lax.broadcasted_iota(jnp.int32, rows.shape, 0) % 4
    return jnp.where(
        field < 4 - shift,
        pltpu.roll(rows, count - shift, axis=0),
        pltpu.roll(rows, 4 - shift, axis=0),
    )


def build_tables(points_ref, waves_ref, base_cos, base_sin, start_cos, start_sin, cos_tab, sin_tab):
    width = cos_tab.shape[0]
    wave_count = cos_tab.shape[1]
    row_points = points_ref[0]
    quarter_int = row_points // 4
    quarter = quarter_int.astype(jnp.float32)
    step = (0.5 * math.pi) / quarter
    m_int = waves_ref[...]
    m_float = m_int.astype(jnp.float32)

    def start_rows(count, scale):
        return (lax.broadcasted_iota(jnp.int32, (count, 1), 0) * scale).astype(jnp.float32)

    start_cos[...], start_sin[...] = sincos(start_rows(start_cos.shape[0], LANE) * m_float, quarter, step)

    @pl.loop(0, LANE // 8, unroll=2)
    def _(index):
        at = pl.multiple_of(index * 8, 8)
        offsets = (lax.broadcasted_iota(jnp.int32, (8, 1), 0) + at).astype(jnp.float32)
        base_cos[pl.ds(at, 8), :], base_sin[pl.ds(at, 8), :] = sincos(offsets * m_float, quarter, step)

    @pl.loop(0, width // 16, unroll=2)
    def _(index):
        at = pl.multiple_of(index * 16, 16)
        low = pl.multiple_of((index % (LANE // 16)) * 16, 16)
        start = index // (LANE // 16)
        for col in range(0, wave_count, 2 * LANE):
            cols = pl.ds(col, 2 * LANE)
            bc = base_cos[pl.ds(low, 16), cols]
            bs = base_sin[pl.ds(low, 16), cols]
            sc = start_cos[pl.ds(start, 1), cols]
            ss = start_sin[pl.ds(start, 1), cols]
            cos_tab[pl.ds(at, 16), cols] = (sc * bc - ss * bs).astype(jnp.bfloat16)
            sin_tab[pl.ds(at, 16), cols] = (ss * bc + sc * bs).astype(jnp.bfloat16)


def grid_rows(
    points_ref, scales_ref, waves_ref, four_ref, out_ref,
    cos_tab, sin_tab, lhs_cos, lhs_sin, term_cos, term_sin, images,
):
    width, wave_count = cos_tab.shape
    rows = four_ref.shape[1]
    blocks = width // LANE
    row_points = points_ref[0]
    quarter_int = row_points // 4
    m_int = waves_ref[...]
    m_float = m_int.astype(jnp.float32)
    active = 2 * m_int < row_points
    parity = jnp.where((m_int & 1) == 0, 1.0, -1.0)
    factor = jnp.where(active, jnp.where(m_int == 0, 1.0, 2.0), 0.0)
    slope = factor * (m_float * (1.0 / wave_count))
    part_rows = rows // 2

    def rows_of(slope_of, part):
        pieces = [four_ref[2 * row + slope_of].astype(jnp.float32) for row in range(2)]
        return jnp.concatenate([piece[part * part_rows:(part + 1) * part_rows] for piece in pieces], axis=0)

    real_value, imag_value, real_slope, imag_slope = rows_of(0, 0), rows_of(0, 1), rows_of(1, 0), rows_of(1, 1)

    def fill(lhs, value, zonal, merid):
        parts = [value, shift_field(value, 1), shift_field(value, 2), shift_field(value, 3), zonal, merid]
        for index, part in enumerate(parts):
            lhs[pl.ds(index * rows, rows), :] = part.astype(jnp.bfloat16)
            lhs[pl.ds((6 + index) * rows, rows), :] = (part * parity).astype(jnp.bfloat16)

    fill(lhs_cos, factor * real_value, -slope * imag_value, factor * real_slope)
    fill(lhs_sin, -factor * imag_value, -slope * real_value, -factor * imag_slope)
    which_row = lax.broadcasted_iota(jnp.int32, (rows, 1), 0) < part_rows
    scale = jnp.where(which_row, scales_ref[0], scales_ref[1]) / row_points.astype(jnp.float32)

    for index in range(blocks):
        at = index * LANE
        contract = (((1,), (1,)), ((), ()))
        even = lax.dot_general(lhs_cos[...], cos_tab[pl.ds(at, LANE), :], contract, preferred_element_type=jnp.float32)
        odd = lax.dot_general(lhs_sin[...], sin_tab[pl.ds(at, LANE), :], contract, preferred_element_type=jnp.float32)
        place = lax.broadcasted_iota(jnp.int32, (1, LANE), 1) + at
        closed = place <= quarter_int
        inner = (place >= 1) & (place < quarter_int)
        half = 6 * rows
        fields = (
            (even[:half] + odd[:half], closed),
            (even[half:] + odd[half:], closed),
            (even[half:] - odd[half:], inner),
            (even[:half] - odd[:half], inner),
        )
        terms = []
        for image, (field, keep) in enumerate(fields):
            q0, q1, q2, q3, zonal, merid = (field[part * rows:(part + 1) * rows] for part in range(6))
            images[image, :, pl.ds(at, LANE)] = jnp.where(keep, q0, 0.0)
            weight = jnp.where(keep, scale, 0.0)
            terms.append(jnp.concatenate([(q1 * zonal + q2 * merid) * weight, q0 * q3 * weight], axis=0))
        cols = pl.ds(at, LANE)
        term_cos[:, cols] = jnp.concatenate([terms[0] + terms[3], terms[1] + terms[2]], axis=0).astype(jnp.bfloat16)
        term_sin[:, cols] = jnp.concatenate([terms[0] - terms[3], terms[1] - terms[2]], axis=0).astype(jnp.bfloat16)

    keep_wave = jnp.where(active, 1.0, 0.0)
    real = jnp.dot(term_cos[...], cos_tab[...], preferred_element_type=jnp.float32)
    imag = jnp.dot(term_sin[...], sin_tab[...], preferred_element_type=jnp.float32)
    split = 2 * rows
    real = (real[:split] + parity * real[split:]) * keep_wave
    imag = -(imag[:split] + parity * imag[split:]) * keep_wave
    for term in range(2):
        for row in range(2):
            low = term * rows + row * part_rows
            both = [real[low:low + part_rows], imag[low:low + part_rows]]
            out_ref[2 * row + term] = jnp.concatenate(both, axis=0).astype(out_ref.dtype)


def place_values(points_ref, images, values_ref):
    _, rows, width = images.shape
    blocks = width // LANE
    row_points = points_ref[0]
    flip = (
        lax.broadcasted_iota(jnp.int32, (LANE, LANE), 0) + lax.broadcasted_iota(jnp.int32, (LANE, LANE), 1) == LANE - 1
    ).astype(jnp.float32).astype(jnp.bfloat16)
    pad = jnp.zeros((rows, NPAD - width), jnp.float32)

    def reverse(image):
        parts = [
            jnp.dot(images[image, :, pl.ds(block * LANE, LANE)].astype(jnp.bfloat16), flip, preferred_element_type=jnp.float32)
            for block in reversed(range(blocks))
        ]
        return jnp.concatenate(parts + [pad], axis=1)

    def straight(image):
        return jnp.concatenate([images[image], pad], axis=1)

    halfway = row_points // 2
    total = straight(0)
    total = total + pltpu.roll(straight(1), halfway, axis=1)
    total = total + pltpu.roll(reverse(2), lax.rem(halfway - (width - 1) + NPAD, NPAD), axis=1)
    total = total + pltpu.roll(reverse(3), lax.rem(row_points - (width - 1) + NPAD, NPAD), axis=1)
    for row in range(values_ref.shape[0]):
        for level in range(values_ref.shape[1]):
            low = (row * values_ref.shape[1] + level) * 4
            values_ref[row, level] = total[low:low + 4].astype(values_ref.dtype)


def split_column(column):
    return (column // 4 % 2) * 8 + column // 8 * 4 + column % 4


def greet(lat_size, lev_size):
    lat, lev = lax.axis_index("lat"), lax.axis_index("lev")
    barrier = pltpu.get_barrier_semaphore()
    for hop in range(1, lev_size):
        pl.semaphore_signal(barrier, inc=1, device_id=(lat, lax.rem(lev + hop, lev_size)), device_id_type=pl.DeviceIdType.MESH)
    for hop in range(1, lat_size):
        pl.semaphore_signal(barrier, inc=1, device_id=(lax.rem(lat + hop, lat_size), lev), device_id_type=pl.DeviceIdType.MESH)
    pl.semaphore_wait(barrier, lat_size + lev_size - 2)


def remote(src, dst, send_sem, recv_sem, device):
    return pltpu.make_async_remote_copy(
        src_ref=src, dst_ref=dst, send_sem=send_sem, recv_sem=recv_sem,
        device_id=device, device_id_type=pl.DeviceIdType.MESH,
    )


def transform_kernel(
    lat_size, lev_size, pack, chunks,
    own_ref, points_ref, scales_ref, waves_ref, spec_hbm, leg_hbm, out_ref, images,
    spec, leg, lev_send, lev_recv, summed, turned, lat_send, lat_recv,
    load_sem, lev_send_sem, lev_recv_sem, lat_send_sem, lat_recv_sem,
    four, wave_rows, base_cos, base_sin, start_cos, start_sin, cos_tab, sin_tab,
    lhs_cos, lhs_sin, term_cos, term_sin,
    back_send, back_recv, back_turned, grouped, all_send, all_recv,
    back_send_sem, back_recv_sem, all_send_sem, all_recv_sem,
):
    lat, lev = lax.axis_index("lat"), lax.axis_index("lev")
    _, groups, columns, totals = spec.shape
    rows = leg.shape[2]
    size = groups // chunks
    loads = []
    for chunk in range(chunks):
        part = pl.ds(chunk * size, size)
        pair = [
            pltpu.make_async_copy(spec_hbm.at[:, part], spec.at[:, part], load_sem.at[chunk, 0]),
            pltpu.make_async_copy(leg_hbm.at[:, part], leg.at[:, part], load_sem.at[chunk, 1]),
        ]
        for copy in pair:
            copy.start()
        loads.append(pair)
    greet(lat_size, lev_size)
    number = lax.broadcasted_iota(jnp.int32, (1, totals), 1) + lev * totals
    lane = lax.broadcasted_iota(jnp.int32, (1, pack * rows), 1) // rows
    share = columns // lev_size
    copies = []
    for chunk in range(chunks):
        for copy in loads[chunk]:
            copy.wait()

        @pl.loop(chunk * size, (chunk + 1) * size, unroll=4)
        def _(group):
            tables = []
            for which in range(pack):
                kept = jnp.where(number >= own_ref[lat * pack * groups + which * groups + group], 1.0, 0.0).astype(jnp.bfloat16)
                tables.append(leg[which, group] * kept)
            table = jnp.concatenate(tables, axis=0)
            source = jnp.concatenate([spec[which, group] for which in range(pack)], axis=0)
            product = lax.dot_general(source, table, (((1,), (1,)), ((), ())), preferred_element_type=jnp.float32)
            result = product[:columns]
            for which in range(1, pack):
                result = jnp.where(lane == which, product[which * columns:(which + 1) * columns], result)
            result = result.astype(jnp.bfloat16)
            for peer in range(lev_size):
                lev_send[peer, group] = result[peer * share:(peer + 1) * share]

        part = pl.ds(chunk * size, size)
        for hop in range(1, lev_size):
            peer = lax.rem(lev + hop, lev_size)
            copy = remote(
                lev_send.at[peer, part], lev_recv.at[hop - 1, part],
                lev_send_sem.at[chunk, hop - 1], lev_recv_sem.at[chunk, hop - 1], (lat, peer),
            )
            copy.start()
            copies.append(copy)
    build_tables(points_ref, waves_ref, base_cos, base_sin, start_cos, start_sin, cos_tab, sin_tab)
    for chunk in range(chunks):
        for hop in range(1, lev_size):
            copies[chunk * (lev_size - 1) + hop - 1].wait_recv()
        part = pl.ds(chunk * size, size)
        total = lev_send[lev, part].astype(jnp.float32)
        for hop in range(1, lev_size):
            total = total + lev_recv[hop - 1, part].astype(jnp.float32)
        summed[part] = total
    for column in range(share):
        flat = jnp.transpose(summed[:, column, :])
        turned[:, split_column(column), :] = jnp.concatenate(
            [flat[which * rows:(which + 1) * rows] for which in range(pack)], axis=1
        )
    lat_send[...] = turned[...].astype(jnp.bfloat16)
    block = rows // lat_size
    swaps = []
    for hop in range(1, lat_size):
        peer = lax.rem(lat + hop, lat_size)
        copy = remote(
            lat_send.at[pl.ds(peer * block, block)], lat_recv.at[lat],
            lat_send_sem.at[hop - 1], lat_recv_sem.at[hop - 1], (peer, lev),
        )
        copy.start()
        swaps.append(copy)
    lat_recv[lat] = lat_send[pl.ds(lat * block, block)]
    for copy in copies:
        copy.wait_send()
    for copy in swaps:
        copy.wait()
    for row in range(block):
        pieces = [lat_recv[source, row].astype(jnp.float32) for source in range(lat_size)]
        four[row] = jnp.concatenate(pieces, axis=1).astype(jnp.bfloat16)
    grid_rows(
        points_ref, scales_ref, waves_ref, four, wave_rows,
        cos_tab, sin_tab, lhs_cos, lhs_sin, term_cos, term_sin, images,
    )
    direct_steps(
        lat_size, lev_size, pack, wave_rows, out_ref,
        back_send, back_recv, back_turned, grouped, all_send, all_recv,
        back_send_sem, back_recv_sem, all_send_sem, all_recv_sem,
    )


def direct_steps(
    lat_size, lev_size, pack,
    waves_ref, out_ref,
    lat_send, lat_recv, turned, grouped, lev_send, lev_recv,
    lat_send_sem, lat_recv_sem, lev_send_sem, lev_recv_sem,
):
    lat, lev = lax.axis_index("lat"), lax.axis_index("lev")
    block, share, _ = waves_ref.shape
    own = lat_send.shape[3]
    rows, groups = lat_size * block, own // pack
    for row in range(block):
        line = waves_ref[row].astype(jnp.float32)
        for peer in range(lat_size):
            lat_send[peer, row] = line[:, peer * own:(peer + 1) * own].astype(jnp.bfloat16)
    swaps = []
    for hop in range(1, lat_size):
        peer = lax.rem(lat + hop, lat_size)
        copy = remote(lat_send.at[peer], lat_recv.at[lat], lat_send_sem.at[hop - 1], lat_recv_sem.at[hop - 1], (peer, lev))
        copy.start()
        swaps.append(copy)
    lat_recv[lat] = lat_send[lat]
    for copy in swaps:
        copy.wait()
    turned[...] = lat_recv[...].astype(jnp.float32).reshape(rows, share, own)
    for column in range(share):
        line = turned[:, split_column(column), :]
        flat = jnp.concatenate([line[:, which * groups:(which + 1) * groups] for which in range(pack)], axis=0)
        grouped[:, column, :] = jnp.transpose(flat)
    lev_send[...] = grouped[...].astype(jnp.bfloat16)
    twin = lev + 1 - 2 * lax.rem(lev, 2)
    far, near = [], []
    half = groups // 2
    for part in range(2):
        for hop in range(1, lev_size // 2):
            peer = lax.rem(lev + 2 * hop, lev_size)
            index = part * (lev_size // 2) + hop
            rows_of = pl.ds(part * half, half)
            copy = remote(
                lev_send.at[rows_of], lev_recv.at[lev, rows_of],
                lev_send_sem.at[0, index], lev_recv_sem.at[0, index], (lat, peer),
            )
            copy.start()
            far.append((copy, hop, index, rows_of))
    copy = remote(lev_send, lev_recv.at[lev], lev_send_sem.at[1, 0], lev_recv_sem.at[1, 0], (lat, twin))
    copy.start()
    near.append(copy)
    lev_recv[lev] = lev_send[...]
    for copy, hop, index, rows_of in far:
        copy.wait_recv()
        source = lax.rem(lev - 2 * hop + lev_size, lev_size)
        passed = remote(
            lev_recv.at[source, rows_of], lev_recv.at[source, rows_of],
            lev_send_sem.at[1, index], lev_recv_sem.at[1, index], (lat, twin),
        )
        passed.start()
        near.append(passed)
    for copy, _, _, _ in far:
        copy.wait_send()
    for copy in near:
        copy.wait()
    out_ref[...] = lev_recv[...]


def tendency_kernel(own_ref, points_ref, waves_ref, leg_ref, images, out_ref, values_ref):
    pack, size, rows, totals = leg_ref.shape
    groups = size * pl.num_programs(0)
    lev_size, _, share, lanes = waves_ref.shape
    columns = lev_size * share
    first = pl.program_id(0) * size
    lat = lax.axis_index("lat")
    number = lax.broadcasted_iota(jnp.int32, (1, totals), 1) + lax.axis_index("lev") * totals
    lane = lax.broadcasted_iota(jnp.int32, (1, lanes), 1) // rows

    @pl.when(pl.program_id(0) == 0)
    def _():
        place_values(points_ref, images, values_ref)

    @pl.loop(0, size, unroll=4)
    def _(group):
        waves = jnp.concatenate([waves_ref[peer, group] for peer in range(lev_size)], axis=0)
        spread = jnp.concatenate(
            [waves * jnp.where(lane == which, 1.0, 0.0).astype(jnp.bfloat16) for which in range(pack)], axis=0
        )
        table = jnp.concatenate([leg_ref[which, group] for which in range(pack)], axis=0)
        product = jnp.dot(spread, table, preferred_element_type=jnp.float32)
        for which in range(pack):
            kept = number >= own_ref[lat * pack * groups + which * groups + first + group]
            out_ref[which, group] = jnp.where(kept, product[which * columns:(which + 1) * columns], 0.0).astype(jnp.bfloat16)


def body(spectral, legendre, weights, points, assignment):
    own_slots, own_totals, column_count = spectral.shape
    wave_count = assignment.shape[0]
    rows = legendre.shape[2]
    levels = column_count // 8
    lat_size, lev_size = lax.axis_size("lat"), lax.axis_size("lev")
    local_levels = levels // lev_size
    share = column_count // lev_size
    pack = LANE // rows
    groups = own_slots // pack
    block = rows // lat_size
    chunks = 5
    spec_in = jnp.transpose(spectral, (0, 2, 1)).reshape(pack, groups, column_count, own_totals)
    leg_in = jnp.transpose(legendre, (0, 2, 1)).reshape(pack, groups, rows, own_totals)
    smem, vmem = pl.BlockSpec(memory_space=pltpu.SMEM), pl.BlockSpec(memory_space=pltpu.VMEM)
    anywhere = pl.BlockSpec(memory_space=pl.ANY)
    f32, b16 = jnp.float32, jnp.bfloat16
    dma = pltpu.SemaphoreType.DMA
    width = -(-(wave_count + 5) // LANE) * LANE
    starts = -(-(width // LANE) // 8) * 8
    gathered, images = pl.pallas_call(
        functools.partial(transform_kernel, lat_size, lev_size, pack, chunks),
        out_shape=(
            jax.ShapeDtypeStruct((lev_size, groups, share, pack * rows), b16),
            jax.ShapeDtypeStruct((4, share, width), f32),
        ),
        in_specs=[smem, smem, smem, vmem, anywhere, anywhere],
        out_specs=(vmem, vmem),
        scratch_shapes=[
            pltpu.VMEM((pack, groups, column_count, own_totals), b16),
            pltpu.VMEM((pack, groups, rows, own_totals), b16),
            pltpu.VMEM((lev_size, groups, share, pack * rows), b16),
            pltpu.VMEM((lev_size - 1, groups, share, pack * rows), b16),
            pltpu.VMEM((groups, share, pack * rows), f32),
            pltpu.VMEM((rows, share, own_slots), f32),
            pltpu.VMEM((rows, share, own_slots), b16),
            pltpu.VMEM((lat_size, block, share, own_slots), b16),
            dma((chunks, 2)), dma((chunks, lev_size - 1)), dma((chunks, lev_size - 1)),
            dma((lat_size - 1,)), dma((lat_size - 1,)),
            pltpu.VMEM((block, share, wave_count), b16),
            pltpu.VMEM((block, share, wave_count), b16),
            pltpu.VMEM((LANE, wave_count), f32),
            pltpu.VMEM((LANE, wave_count), f32),
            pltpu.VMEM((starts, wave_count), f32),
            pltpu.VMEM((starts, wave_count), f32),
            pltpu.VMEM((width, wave_count), b16),
            pltpu.VMEM((width, wave_count), b16),
            pltpu.VMEM((12 * share, wave_count), b16),
            pltpu.VMEM((12 * share, wave_count), b16),
            pltpu.VMEM((4 * share, width), b16),
            pltpu.VMEM((4 * share, width), b16),
            pltpu.VMEM((lat_size, block, share, own_slots), b16),
            pltpu.VMEM((lat_size, block, share, own_slots), b16),
            pltpu.VMEM((rows, share, own_slots), f32),
            pltpu.VMEM((groups, share, pack * rows), f32),
            pltpu.VMEM((groups, share, pack * rows), b16),
            pltpu.VMEM((lev_size, groups, share, pack * rows), b16),
            dma((lat_size - 1,)), dma((lat_size - 1,)), dma((2, lev_size)), dma((2, lev_size)),
        ],
        compiler_params=pltpu.CompilerParams(
            collective_id=0, has_side_effects=True, vmem_limit_bytes=60 * 1024 * 1024
        ),
    )(assignment, points, weights, assignment[None, :], spec_in, leg_in)
    size = groups // 5
    result, values = pl.pallas_call(
        tendency_kernel,
        grid=(groups // size,),
        out_shape=(
            jax.ShapeDtypeStruct((pack, groups, column_count, own_totals), b16),
            jax.ShapeDtypeStruct((2, local_levels, 4, NPAD), b16),
        ),
        in_specs=[
            smem,
            smem,
            pl.BlockSpec((lev_size, size, share, pack * rows), lambda step: (0, step, 0, 0)),
            pl.BlockSpec((pack, size, rows, own_totals), lambda step: (0, step, 0, 0)),
            vmem,
        ],
        out_specs=(
            pl.BlockSpec((pack, size, column_count, own_totals), lambda step: (0, step, 0, 0)),
            vmem,
        ),
        compiler_params=pltpu.CompilerParams(vmem_limit_bytes=60 * 1024 * 1024),
    )(assignment, points, gathered, leg_in, images)
    tendency = jnp.transpose(result.reshape(own_slots, column_count, own_totals), (0, 2, 1))
    return (tendency, values)


def solution(mesh):
    in_specs = (P("lat", "lev", None), P("lat", "lev", None), P("lat"), P("lat"), P())
    out_specs = (P("lat", "lev", None), P("lat", "lev", None, None))
    return jax.shard_map(body, mesh=mesh, in_specs=in_specs, out_specs=out_specs, check_vma=False)
```
